512 devices in a mesh: grp: 16 (over z), row: 32 (over y, x, core).
Axes of the slice: x: 4, y: 4, z: 16, core: 2. Of those that a mesh axis runs over, the one named last changes fastest.
Arguments:
- features: bfloat16 [131072, 1024], P(('grp', 'row')), may hold values from -6 to 6
- history: bfloat16 [196608, 1024], P(('grp', 'row')), may hold values from -6 to 6
- weight: bfloat16 [1024, 1024], replicated, may hold values from -3 to 3
- in_tiles: bfloat16 [16, 64, 8, 128, 128], P('grp', 'row'), may hold values from 0 to 9, as said below
- in_cols: int32 [16, 64, 8], P('grp', 'row'), may hold values from 0 to 63, as said below
- tile_live: int32 [16, 64], P('grp', 'row'), may hold values from 1 to 8, 341 in all within a row
- hist_tiles: bfloat16 [16, 64, 8, 128, 128], P('grp', 'row'), may hold values from 0 to 9, as said below
- hist_owner: int32 [8192, 1], P(('grp', 'row')), may hold values from 0 to 15; in each aligned block of 16 rows (0 to 15, 16 to 31, ...) at most 2 rows name the same one
- hist_block: int32 [8192, 1], P(('grp', 'row')), may hold values from 0 to 2
Outputs:
- node_out: bfloat16 [131072, 1024], P(('grp', 'row'))
The draws below stay inside these ranges and needn't reach their ends.
Inputs may be any that keep to these rules, and one draw needn't show every extreme that they name: `in_cols`: slot t of row block b names a column block of the same group within 6 blocks of b; slot 0 names b itself, the other slots distinct offsets, cut to the group's blocks at its ends. Only the first tile_live slots of a row block are tiles of the graph; a group's counts sum to 341. `hist_owner`: among the 16 requests of one device's rows at most 2 name one group, a bound that some block reaches. `in_tiles`: Positive. `hist_tiles`: Positive.
All inputs are finite; a program needn't handle non-finite values.
Results may differ from the reference program's by a relative error of at most 0.0049.
Values may be sent and summed in bfloat16 or wider, within the bound.
A program may use at most 128 MiB of HBM per device.

```python
import math
import jax
import jax.numpy as jnp
import numpy as np
from jax import lax

D = 1024
TILE = 128
BLK_DEV = 2
BAND = 6
TPB = 8
HTB = 8
HB = 3
BLK_GRP = 64
NODES = 131072
HIST = 196608
HT = 16
CAP = 2
N_GRP = 16
N_ROW = 32


def tile_values(key, slots, power):
    key_base, key_rows, key_cols, key_tiles = jax.random.split(key, 4)
    shape = (N_GRP, BLK_GRP, slots, TILE, TILE)
    base = jax.random.uniform(key_base, shape, jnp.float32, 0.05, 1.0) ** power
    row_scale = jnp.exp(jax.random.uniform(key_rows, (N_GRP, BLK_GRP, slots, TILE, 1), jnp.float32, math.log(0.3), math.log(3.0)))
    column_scale = jnp.exp(jax.random.uniform(key_cols, (N_GRP, BLK_GRP, slots, 1, TILE), jnp.float32, math.log(0.3), math.log(3.0)))
    tile_scale = jnp.exp(jax.random.uniform(key_tiles, (N_GRP, BLK_GRP, slots, 1, 1), jnp.float32, math.log(0.1), 0.0))
    return base * row_scale * column_scale * tile_scale


def draw_in_tiles(key, part):
    key = jax.random.fold_in(key, 11)
    power = 2.0
    return tile_values(key, TPB, power).astype(jnp.bfloat16)


def draw_hist_tiles(key, part):
    key = jax.random.fold_in(key, 12)
    power = 2.0
    return tile_values(key, HTB, power).astype(jnp.bfloat16)


def draw_in_cols(key, part):
    key = jax.random.fold_in(key, 13)
    subkeys = jax.random.split(key, N_GRP * BLK_GRP)

    def pick_offsets(subkey):
        shuffled = jax.random.permutation(subkey, 2 * BAND)
        return shuffled[:TPB - 1]
    picks = jax.vmap(pick_offsets)(subkeys).reshape(N_GRP, BLK_GRP, TPB - 1).astype(jnp.int32)
    offsets = jnp.where(picks < BAND, picks - BAND, picks - BAND + 1)
    offsets = jnp.concatenate([jnp.zeros((N_GRP, BLK_GRP, 1), jnp.int32), offsets], axis=2)
    position = jnp.arange(BLK_GRP, dtype=jnp.int32)[None, :, None]
    return jnp.clip(position + offsets, 0, BLK_GRP - 1).astype(jnp.int32)


def set_ends(array, key, least, high):
    index_at = [jax.random.randint(jax.random.fold_in(key, axis), (), 0, length) for axis, length in enumerate(array.shape)]
    main_axis = array.shape.index(max(array.shape))
    neighbour = index_at[:main_axis] + [(index_at[main_axis] + 1) % array.shape[main_axis]] + index_at[main_axis + 1:]
    return array.at[tuple(index_at)].set(least).at[tuple(neighbour)].set(high)


def shard_levels(rng, shape, pieces, low, high):
    gain, own = 1.0, jax.random.fold_in(rng, 6)
    for dim, blocks in pieces:
        heights = jnp.exp(jax.random.uniform(jax.random.fold_in(own, dim), (blocks,), jnp.float32, low / len(pieces), high / len(pieces)))
        gain = gain * jnp.repeat(heights, shape[dim] // blocks).reshape([-1 if axis == dim else 1 for axis in range(len(shape))])
    return gain


def split_up(number_of, total, limit, lean):
    portions = [(1 << 20) // math.isqrt(standing ** lean) + 1 for standing in range(2, number_of + 1)]
    spare, given = total - limit - (number_of - 1), [1] * (number_of - 1)
    while spare > 0:
        free = [i for i in range(number_of - 1) if given[i] < limit]
        mass, budget = sum([portions[i] for i in free]), spare
        for i in free:
            extra = min(limit - given[i], max(1, budget * portions[i] // mass), spare)
            given[i] = given[i] + extra
            spare = spare - extra
    return np.array([limit] + given)


def ragged(rng, amount, total, bound, slope):
    if amount == 2:
        one = jax.random.randint(rng, (), max(1, total - bound), min(bound, total - 1) + 1)
        return jnp.stack([one, total - one])
    sizes = jnp.asarray(split_up(amount, total, bound, slope), jnp.int32)
    couples = (amount - 1) // 2
    giver, sink = sizes[1:1 + 2 * couples:2], sizes[2:2 + 2 * couples:2]
    room = jnp.minimum(giver - 1, bound - sink)
    passed = jax.random.randint(jax.random.fold_in(rng, 1), (couples,), 0, 1 << 20) % (room + 1)
    sizes = sizes.at[1:1 + 2 * couples:2].set(giver - passed).at[2:2 + 2 * couples:2].set(sink + passed)
    return sizes[jax.random.permutation(jax.random.fold_in(rng, 2), amount)]


def shared_out(own_key, own, number, rows, number_of, top, limit, lean):
    sequence = jax.random.permutation(own_key, number_of)
    heavy_load, ordinary = load_shares(number_of, rows * top, limit, lean, True), load_shares(number_of, rows * top, limit, lean, False)
    places = jnp.arange(number_of)

    def named(tallies, offset_by):
        used = int((tallies > 0).sum())
        fixed = max(1, used // 4)
        passed = fixed + (places - fixed + offset_by * (used - fixed)) % max(1, number_of - fixed)
        return jnp.zeros((number_of,), jnp.int32).at[sequence[jnp.where(places < fixed, places, passed)]].set(jnp.asarray(tallies, jnp.int32))

    tallies = jnp.where(number % 4 == 0, named(heavy_load, number // 4), named(ordinary, number - number // 4 - 1))
    mixed = jax.random.permutation(jax.random.fold_in(own, 3), number_of)
    donor, receiver = mixed[0:number_of // 2 * 2:2], mixed[1:number_of // 2 * 2:2]
    margin = jnp.minimum(tallies[donor] - 1, limit - tallies[receiver]) // 2
    margin = jnp.where((donor == sequence[0]) | (receiver == sequence[0]) | (tallies[receiver] == 0), 0, jnp.maximum(margin, 0))
    passed = jax.random.randint(jax.random.fold_in(own, 4), (number_of // 2,), 0, 1 << 20) % (margin + 1)
    tallies = tallies.at[donor].add(-passed).at[receiver].add(passed)
    labels = jnp.searchsorted(jnp.cumsum(tallies), jnp.arange(rows * top), side="right").astype(jnp.int32)
    listing = labels.reshape(top, rows).T
    listing = listing[jax.random.permutation(jax.random.fold_in(own, 1), rows)]
    offset_by = jax.random.randint(jax.random.fold_in(own, 2), (rows, 1), 0, top)
    return jnp.take_along_axis(listing, (jnp.arange(top)[None, :] + offset_by) % top, axis=1)


def load_shares(count, total, limit, skew, full):
    loads = [(1 << 20) // math.isqrt(grade ** skew) + 1 for grade in range(1, count + 1)]
    largest = limit if full else min(limit, max(-(-total // count), total * loads[0] // sum(loads)))
    least = 1 if total - largest >= count - 1 else 0
    counts, surplus = [largest] + [least] * (count - 1), total - largest - least * (count - 1)
    while surplus > 0:
        movable = [i for i in range(1, count) if counts[i] < largest] or [i for i in range(1, count) if counts[i] < limit]
        pool, left = sum([loads[i] for i in movable]), surplus
        for i in movable:
            addition = min(limit - counts[i], max(1, left * loads[i] // pool), surplus)
            counts[i] = counts[i] + addition
            surplus = surplus - addition
    return np.array(counts)


def bell_draw(stream_key, shape, width, reach, cuts=(), kind=jnp.bfloat16):
    factor_of = shard_levels(stream_key, shape, cuts, -0.22, 0.18) if cuts else 1.0
    drawn = jax.random.normal(stream_key, shape, jnp.float32) * width * factor_of
    return jnp.minimum(jnp.maximum(drawn, -reach), reach).astype(kind)


def setup_inputs(seed: int = 0) -> dict:
    streams_of = jax.random.split(jax.random.key(seed), 10)
    features = bell_draw(streams_of[0], (NODES, D), 1.0, 6.0, ((0, 512),))
    history = bell_draw(streams_of[1], (HIST, D), 1.0, 6.0, ((0, 512),))
    weight = bell_draw(streams_of[2], (D, D), (max(1, D // 256)) ** -0.5, 3.0)
    in_tiles = draw_in_tiles(jax.random.fold_in(streams_of[9], 71), 0)
    in_cols = draw_in_cols(jax.random.fold_in(streams_of[9], 71), 0)
    tile_live = jax.vmap(lambda own: ragged(own, BLK_GRP, BLK_GRP * TPB * 2 // 3, TPB, 2))(jax.random.split(streams_of[5], N_GRP)).reshape((N_GRP, BLK_GRP)).astype(jnp.int32)
    hist_tiles = draw_hist_tiles(jax.random.fold_in(streams_of[9], 71), 0)
    hist_owner_keys = jax.random.split(jax.random.fold_in(streams_of[7], 1), (N_GRP * BLK_GRP * HTB) // HT)
    hist_owner_turns = jax.random.permutation(jax.random.fold_in(streams_of[7], 3), (N_GRP * BLK_GRP * HTB) // HT)
    hist_owner = jax.vmap(lambda own, number: shared_out(jax.random.fold_in(streams_of[7], 2), own, number, HT, N_GRP, 1, CAP, 2))(hist_owner_keys, hist_owner_turns).reshape((N_GRP * BLK_GRP * HTB, 1))
    hist_block = set_ends(jax.random.randint(streams_of[8], (N_GRP * BLK_GRP * HTB, 1), 0, HB), jax.random.fold_in(streams_of[8], 1), 0, HB - 1).astype(jnp.int32)
    return dict(features=features, history=history, weight=weight, in_tiles=in_tiles, in_cols=in_cols, tile_live=tile_live, hist_tiles=hist_tiles, hist_owner=hist_owner, hist_block=hist_block)


def reference(features, history, weight, in_tiles, in_cols, tile_live, hist_tiles, hist_owner, hist_block):
    feat_blocks = features.reshape(N_GRP, BLK_GRP, TILE, D)
    hist_rows = history.reshape(N_GRP * N_ROW * HB, TILE, D)
    owner_ids = hist_owner.reshape(N_GRP, BLK_GRP, HTB)
    local_ids = hist_block.reshape(N_GRP, BLK_GRP, HTB)
    device_row = (jnp.arange(BLK_GRP, dtype=jnp.int32) // BLK_DEV)[None, :, None]
    hist_index = ((owner_ids * N_ROW + device_row) * HB + local_ids).astype(jnp.int32)
    slot_live = (jnp.arange(TPB, dtype=jnp.int32)[None, None, :] < tile_live[:, :, None]).astype(jnp.float32)

    def one_group(members):
        blocks, tile_vals, column_ids, live_mask, far_vals, far_index = members

        def one_block(entries):
            near_tiles, near_cols, near_live, far_tiles, far_ids = entries
            near_data = blocks[near_cols].astype(jnp.float32)
            far_data = hist_rows[far_ids].astype(jnp.float32)
            near_f = near_tiles.astype(jnp.float32) * near_live[:, None, None]
            far_f = far_tiles.astype(jnp.float32)
            totals = jnp.einsum("tij,tjd->id", near_f, near_data) + jnp.einsum("tij,tjd->id", far_f, far_data)
            weight_sum = jnp.sum(near_f, axis=(0, 2)) + jnp.sum(far_f, axis=(0, 2))
            return (totals / weight_sum[:, None]).astype(jnp.bfloat16)

        return lax.map(one_block, (tile_vals, column_ids, live_mask, far_vals, far_index))

    mean_rows = lax.map(one_group, (feat_blocks, in_tiles, in_cols, slot_live, hist_tiles, hist_index))
    mean_rows = mean_rows.reshape(NODES, D)
    return jax.nn.relu(jnp.dot(mean_rows, weight, preferred_element_type=jnp.float32)).astype(jnp.bfloat16)
```

```python
import functools

import jax
import jax.numpy as jnp
from jax import lax
from jax.experimental import pallas as pl
from jax.experimental.pallas import tpu as pltpu
from jax.sharding import PartitionSpec as P

MESH = pl.DeviceIdType.MESH
BAND = 6
COLS = 256


def kernel(
    n_grp, n_row, reach,
    cols_ref, live_ref, owner_ref, block_ref,
    feat, hist, weight, near_in, far_in,
    out,
    ring, window, w_buf, near_t, far_t, acc, inv, out_buf,
    load_sem, z_send, z_recv, last_send, last_recv, row_send, row_recv,
):
    g = lax.axis_index("grp")
    r = lax.axis_index("row")
    half = n_grp // 2
    tile = near_t.shape[1]
    width = feat.shape[2]
    blocks = feat.shape[0]
    chunks = hist.shape[0] // tile
    slots = near_t.shape[0] // blocks
    tiles_far = far_t.shape[0] // blocks
    requests = far_t.shape[0]
    shard = hist.shape[0]

    right = lax.rem(g + 1, n_grp)
    left = lax.rem(g + n_grp - 1, n_grp)
    steps = [d for d in range(-reach, reach + 1) if d != 0]

    loads = [
        pltpu.make_async_copy(far_in, far_t, load_sem.at[0]),
        pltpu.make_async_copy(hist, ring.at[0], load_sem.at[1]),
        pltpu.make_async_copy(near_in, near_t, load_sem.at[2]),
        pltpu.make_async_copy(
            feat, window.at[pl.ds(reach * blocks, blocks)], load_sem.at[3]
        ),
        pltpu.make_async_copy(weight, w_buf, load_sem.at[4]),
    ]
    for load in loads:
        load.start()

    barrier = pltpu.get_barrier_semaphore()
    for z in (left, right):
        pl.semaphore_signal(barrier, inc=1, device_id=(z, r), device_id_type=MESH)
    for d in steps:
        pl.semaphore_signal(
            barrier, inc=1, device_id=(g, lax.rem(r + d + n_row, n_row)), device_id_type=MESH
        )
    pl.semaphore_wait(barrier, 2 + len(steps))

    def slot_of(direction, k):
        return k if direction == 0 else half + k

    def chunk_of(direction, c):
        return c if direction == 0 else chunks - 1 - c

    def z_copy(direction, k, c, own=False):
        piece = chunk_of(direction, c)
        rows = pl.ds(piece * tile, tile)
        slot = slot_of(direction, k)
        return pltpu.make_async_remote_copy(
            src_ref=hist.at[rows] if own else ring.at[slot_of(direction, k - 1), rows],
            dst_ref=ring.at[slot, rows],
            send_sem=z_send.at[slot, piece],
            recv_sem=z_recv.at[slot, piece],
            device_id=(right if direction == 0 else left, r),
            device_id_type=MESH,
        )

    def last_pieces(direction):
        first, stop = (0, shard // 2) if direction == 0 else (shard // 2, shard)
        pieces = []
        for c in range(chunks):
            piece = chunk_of(direction, c)
            low, high = max(first, piece * tile), min(stop, piece * tile + tile)
            if low < high:
                pieces.append((c, low, high - low))
        return pieces

    def last_copy(direction, index):
        _, low, size = last_pieces(direction)[index]
        rows = pl.ds(low, size)
        return pltpu.make_async_remote_copy(
            src_ref=ring.at[slot_of(direction, half - 1), rows],
            dst_ref=ring.at[half, rows],
            send_sem=last_send.at[direction, index],
            recv_sem=last_recv.at[direction, index],
            device_id=(right if direction == 0 else left, r),
            device_id_type=MESH,
        )

    def row_copy(d):
        i = steps.index(d)
        return pltpu.make_async_remote_copy(
            src_ref=feat,
            dst_ref=window.at[pl.ds((reach - d) * blocks, blocks)],
            send_sem=row_send.at[i],
            recv_sem=row_recv.at[i],
            device_id=(g, lax.rem(r + d + n_row, n_row)),
            device_id_type=MESH,
        )

    for c in range(chunks):
        for direction in (0, 1):
            z_copy(direction, 1, c, own=True).start()
    for d in steps:
        row_copy(d).start()

    def far_slot(slot, source):
        count = jnp.int32(0)
        first = jnp.int32(0)
        second = jnp.int32(0)
        first_block = jnp.int32(0)
        second_block = jnp.int32(0)
        for h in range(requests):
            named = (owner_ref[h] == source).astype(jnp.int32)
            to_first = named * (count == 0).astype(jnp.int32)
            to_second = named * (count == 1).astype(jnp.int32)
            first = first + to_first * h
            second = second + to_second * h
            first_block = first_block + to_first * block_ref[h]
            second_block = second_block + to_second * block_ref[h]
            count = count + named
        picked = []
        for index, block, least in ((first, first_block, 0), (second, second_block, 1)):
            values = far_t[index].astype(jnp.float32)
            alive = count > least
            parts = []
            for b in range(blocks):
                mine = alive & (index >= b * tiles_far) & (index < (b + 1) * tiles_far)
                parts.append((values * mine.astype(jnp.float32)).astype(jnp.bfloat16))
            picked.append((jnp.concatenate(parts, axis=0), block))
        lhs = jnp.concatenate([part for part, _ in picked], axis=1)

        @pl.loop(0, width // COLS)
        def _(j):
            where = pl.ds(pl.multiple_of(j * COLS, COLS), COLS)
            data = [ring[slot, pl.ds(p * tile, tile), where] for p in range(chunks)]
            taken = []
            for _, block in picked:
                number = jnp.full((tile, COLS), block, jnp.int32)
                value = data[0]
                for p in range(1, chunks):
                    value = jnp.where(number == p, data[p], value)
                taken.append(value)
            rhs = jnp.concatenate(taken, axis=0)
            acc[:, where] += jnp.dot(lhs, rhs, preferred_element_type=jnp.float32)

    def near_block(b):
        live = live_ref[0, b]
        start = (r - reach) * blocks
        rows = pl.ds(b * tile, tile)
        for t in range(0, slots, 2):
            lhs = jnp.concatenate(
                [
                    (
                        near_t[b * slots + u].astype(jnp.float32)
                        * (u < live).astype(jnp.float32)
                    ).astype(jnp.bfloat16)
                    for u in (t, t + 1)
                ],
                axis=1,
            )
            places = [
                jnp.clip(cols_ref[0, b, u] - start, 0, (2 * reach + 1) * blocks - 1)
                for u in (t, t + 1)
            ]

            @pl.loop(0, width // COLS)
            def _(j):
                where = pl.ds(pl.multiple_of(j * COLS, COLS), COLS)
                rhs = jnp.concatenate(
                    [window[p, :, where] for p in places],
                    axis=0,
                )
                acc[rows, where] += jnp.dot(lhs, rhs, preferred_element_type=jnp.float32)

    acc[...] = jnp.zeros_like(acc)
    loads[0].wait()
    loads[1].wait()
    far_slot(0, g)

    loads[2].wait()
    for b in range(blocks):
        live = live_ref[0, b]
        total = jnp.zeros((tile, tile), jnp.float32)
        for t in range(slots):
            total = total + near_t[b * slots + t].astype(jnp.float32) * (t < live).astype(jnp.float32)
        for h in range(tiles_far):
            total = total + far_t[b * tiles_far + h].astype(jnp.float32)
        sums = jnp.sum(total, axis=1, keepdims=True)
        inv[pl.ds(b * tile, tile), :] = jnp.broadcast_to(1.0 / sums, (tile, tile))

    @pl.loop(1, half - 1)
    def _(k):
        for c in range(chunks):
            for direction in (0, 1):
                z_copy(direction, k, c).wait_recv()
                z_copy(direction, k + 1, c).start()
        far_slot(k, lax.rem(g - k + n_grp, n_grp))
        far_slot(half + k, lax.rem(g + k, n_grp))

    k = half - 1
    for c in range(chunks):
        for direction in (0, 1):
            z_copy(direction, k, c).wait_recv()
            for index, (piece, _, _) in enumerate(last_pieces(direction)):
                if piece == c:
                    last_copy(direction, index).start()
    far_slot(k, lax.rem(g - k + n_grp, n_grp))
    far_slot(half + k, lax.rem(g + k, n_grp))

    loads[3].wait()
    for d in steps:
        row_copy(d).wait()
    for b in range(blocks):
        near_block(b)

    for c in range(chunks):
        for direction in (0, 1):
            z_copy(direction, 1, c, own=True).wait_send()

    @pl.loop(1, half - 1)
    def _(k):
        for c in range(chunks):
            for direction in (0, 1):
                z_copy(direction, k + 1, c).wait_send()

    loads[4].wait()
    for direction in (0, 1):
        for index in range(len(last_pieces(direction))):
            last_copy(direction, index).wait()
    far_slot(half, lax.rem(g + half, n_grp))

    mean = (acc[...] * jnp.concatenate([inv[...]] * (width // tile), axis=1)).astype(jnp.bfloat16)
    @pl.loop(0, width // COLS)
    def _(j):
        where = pl.ds(pl.multiple_of(j * COLS, COLS), COLS)
        full = jnp.dot(mean, w_buf[:, where], preferred_element_type=jnp.float32)
        out_buf[:, where] = jnp.maximum(full, 0.0).astype(jnp.bfloat16)
    store = pltpu.make_async_copy(out_buf, out, load_sem.at[0])
    store.start()
    store.wait()


def solution(mesh):
    n_grp, n_row = mesh.shape["grp"], mesh.shape["row"]

    def body(
        features, history, weight, in_tiles, in_cols, tile_live, hist_tiles, hist_owner, hist_block
    ):
        tile = in_tiles.shape[3]
        rows, width = features.shape
        blocks = rows // tile
        shard = history.shape[0]
        chunks = shard // tile
        reach = (BAND + blocks - 1) // blocks
        near = in_tiles.reshape(-1, tile, tile)
        far = hist_tiles.reshape(-1, tile, tile)
        smem = pl.BlockSpec(memory_space=pltpu.SMEM)
        hbm = pl.BlockSpec(memory_space=pl.ANY)
        return pl.pallas_call(
            functools.partial(kernel, n_grp, n_row, reach),
            out_shape=jax.ShapeDtypeStruct((rows, width), jnp.bfloat16),
            in_specs=[smem] * 4 + [hbm] * 5,
            out_specs=hbm,
            scratch_shapes=[
                pltpu.VMEM((n_grp, shard, width), jnp.bfloat16),
                pltpu.VMEM(((2 * reach + 1) * blocks, tile, width), jnp.bfloat16),
                pltpu.VMEM(weight.shape, jnp.bfloat16),
                pltpu.VMEM(near.shape, jnp.bfloat16),
                pltpu.VMEM(far.shape, jnp.bfloat16),
                pltpu.VMEM((rows, width), jnp.float32),
                pltpu.VMEM((rows, tile), jnp.float32),
                pltpu.VMEM((rows, width), jnp.bfloat16),
                pltpu.SemaphoreType.DMA((5,)),
                pltpu.SemaphoreType.DMA((n_grp, chunks)),
                pltpu.SemaphoreType.DMA((n_grp, chunks)),
                pltpu.SemaphoreType.DMA((2, chunks)),
                pltpu.SemaphoreType.DMA((2, chunks)),
                pltpu.SemaphoreType.DMA((2 * reach,)),
                pltpu.SemaphoreType.DMA((2 * reach,)),
            ],
            compiler_params=pltpu.CompilerParams(
                collective_id=0, has_side_effects=True, vmem_limit_bytes=60 * 1024 * 1024
            ),
        )(
            in_cols, tile_live, hist_owner.reshape(-1), hist_block.reshape(-1),
            features.reshape(-1, tile, width), history, weight, near, far,
        )

    placed = (
        P(("grp", "row"), None),
        P(("grp", "row"), None),
        P(),
        P("grp", "row", None, None, None),
        P("grp", "row", None),
        P("grp", "row"),
        P("grp", "row", None, None, None),
        P(("grp", "row"), None),
        P(("grp", "row"), None),
    )
    return jax.shard_map(
        body, mesh=mesh, in_specs=placed, out_specs=P(("grp", "row"), None), check_vma=False
    )
```

```python
import functools

import jax
import jax.numpy as jnp
from jax import lax
from jax.experimental import pallas as pl
from jax.experimental.pallas import tpu as pltpu
from jax.sharding import PartitionSpec as P

MESH = pl.DeviceIdType.MESH
BAND = 6
COLS = 256


def split_ring(n_grp):
    far = (n_grp - 4) // 4
    ahead = n_grp // 2 - far
    behind = n_grp - 1 - 2 * far - ahead
    return behind, ahead, far


def kernel(
    n_grp, n_row, reach,
    cols_ref, live_ref, owner_ref, block_ref,
    feat, hist, weight, near_in, far_in,
    out,
    ring, window, w_buf, near_t, far_t, acc, inv, mean, out_buf,
    packets, relays, parts, part_send, part_recv,
    load_sem, z_send, z_recv, tile_send, tile_recv, sum_send, sum_recv, row_send, row_recv,
):
    g = lax.axis_index("grp")
    r = lax.axis_index("row")
    behind, ahead, n_far = split_ring(n_grp)
    tile = near_t.shape[1]
    blocks, _, width = feat.shape
    chunks = hist.shape[0] // tile
    slots = near_t.shape[0] // blocks
    tiles_far = far_t.shape[0] // blocks
    requests = far_t.shape[0]
    own = behind
    steps = [d for d in range(-reach, reach + 1) if d != 0]

    sign = 1 - 2 * lax.rem(r, 2)

    def at(distance):
        return lax.rem(g + sign * distance + 2 * n_grp, n_grp)

    def beside(d):
        return lax.rem(r + d + n_row, n_row)

    loads = [
        pltpu.make_async_copy(far_in, far_t, load_sem.at[0]),
        pltpu.make_async_copy(hist, ring.at[own], load_sem.at[1]),
        pltpu.make_async_copy(near_in, near_t, load_sem.at[2]),
        pltpu.make_async_copy(feat, window.at[pl.ds(reach * blocks, blocks)], load_sem.at[3]),
        pltpu.make_async_copy(weight, w_buf, load_sem.at[4]),
    ]
    for load in loads:
        load.start()

    barrier = pltpu.get_barrier_semaphore()
    for j in range(1, n_far + 1):
        for z in (at(-j), at(j)):
            pl.semaphore_signal(barrier, inc=1, device_id=(z, r), device_id_type=MESH)
    for d in steps:
        pl.semaphore_signal(barrier, inc=1, device_id=(g, beside(d)), device_id_type=MESH)
    pl.semaphore_wait(barrier, 2 * n_far + len(steps))

    def slot_of(direction, k):
        return own - k if direction == 0 else own + k

    def towards(direction):
        return at(1) if direction == 0 else at(-1)

    def z_copy(direction, k, c, first=False):
        rows = pl.ds(c * tile, tile)
        slot = slot_of(direction, k)
        return pltpu.make_async_remote_copy(
            src_ref=hist.at[rows] if first else ring.at[slot_of(direction, k - 1), rows],
            dst_ref=ring.at[slot, rows],
            send_sem=z_send.at[slot, c],
            recv_sem=z_recv.at[slot, c],
            device_id=(towards(direction), r),
            device_id_type=MESH,
        )

    def packet_copy(direction, j):
        index = n_far - j if direction == 0 else n_far + own + ahead + j
        return pltpu.make_async_remote_copy(
            src_ref=packets.at[index],
            dst_ref=relays.at[direction, j - 1],
            send_sem=tile_send.at[direction, j - 1],
            recv_sem=tile_recv.at[direction, j - 1],
            device_id=(at(-j) if direction == 0 else at(j), r),
            device_id_type=MESH,
        )

    def sum_copy(direction, h, b):
        return pltpu.make_async_remote_copy(
            src_ref=part_send.at[direction, h - 1, b],
            dst_ref=part_recv.at[direction, h - 1, b],
            send_sem=sum_send.at[direction, h - 1, b],
            recv_sem=sum_recv.at[direction, h - 1, b],
            device_id=(towards(direction), r),
            device_id_type=MESH,
        )

    def row_copy(d):
        i = steps.index(d)
        return pltpu.make_async_remote_copy(
            src_ref=feat,
            dst_ref=window.at[pl.ds((reach - d) * blocks, blocks)],
            send_sem=row_send.at[i],
            recv_sem=row_recv.at[i],
            device_id=(g, beside(d)),
            device_id_type=MESH,
        )

    for c in range(chunks):
        for direction in (0, 1):
            z_copy(direction, 1, c, first=True).start()
    for d in steps:
        row_copy(d).start()

    def pack(i):
        source = at(i - behind - n_far)
        count = jnp.int32(0)
        index = [jnp.int32(0), jnp.int32(0)]
        block = [jnp.int32(0), jnp.int32(0)]
        for h in range(requests):
            named = (owner_ref[h] == source).astype(jnp.int32)
            for c in range(2):
                taken = named * (count == c).astype(jnp.int32)
                index[c] = index[c] + taken * h
                block[c] = block[c] + taken * block_ref[h]
            count = count + named
        marks = []
        for c in range(2):
            alive = (count > c).astype(jnp.float32)
            packets[i, pl.ds(c * tile, tile), :] = (
                far_t[index[c]].astype(jnp.float32) * alive
            ).astype(jnp.bfloat16)
            marks += [index[c] // tiles_far, block[c]]
        row = lax.broadcasted_iota(jnp.int32, (16, tile), 0)
        rows = jnp.zeros((16, tile), jnp.int32)
        for n, mark in enumerate(marks):
            rows = rows + (row == n).astype(jnp.int32) * mark
        packets[i, pl.ds(2 * tile, 16), :] = rows.astype(jnp.float32).astype(jnp.bfloat16)

    def apply(packet, slot, put):
        marks = packet[pl.ds(2 * tile, 16), :].astype(jnp.float32).astype(jnp.int32)
        tops = [[] for _ in range(blocks)]
        numbers = []
        for c in range(2):
            values = packet[pl.ds(c * tile, tile), :].astype(jnp.float32)
            mine = marks[2 * c : 2 * c + 1, :]
            for b in range(blocks):
                keep = (mine == b).astype(jnp.float32)
                tops[b].append((values * keep).astype(jnp.bfloat16))
            numbers.append(
                jnp.broadcast_to(
                    jnp.concatenate([marks[2 * c + 1 : 2 * c + 2, :]] * (COLS // tile), axis=1),
                    (tile, COLS),
                )
            )
        lhs = jnp.concatenate([jnp.concatenate(top, axis=1) for top in tops], axis=0)

        @pl.loop(0, width // COLS)
        def _(j):
            where = pl.ds(pl.multiple_of(j * COLS, COLS), COLS)
            data = [ring[slot, pl.ds(p * tile, tile), where] for p in range(chunks)]
            taken = []
            for number in numbers:
                value = data[0]
                for p in range(1, chunks):
                    value = jnp.where(number == p, data[p], value)
                taken.append(value)
            rhs = jnp.concatenate(taken, axis=0)
            put(where, jnp.dot(lhs, rhs, preferred_element_type=jnp.float32))

    def far_slot(slot):
        def put(where, value):
            acc[:, where] += value

        apply(packets.at[slot + n_far], slot, put)

    def relay_first(direction):
        def put(where, value):
            for b in range(blocks):
                part_send[direction, 0, b, :, where] = value[b * tile : (b + 1) * tile].astype(
                    jnp.bfloat16
                )

        slot = 0 if direction == 0 else own + ahead
        apply(relays.at[direction, n_far - 1], slot, put)
        for b in range(blocks):
            sum_copy(direction, 1, b).start()

    def relay_later(direction):
        for j in range(n_far - 1, 0, -1):
            def put(where, value, j=j):
                parts[direction, j - 1, :, where] = value

            slot = 0 if direction == 0 else own + ahead
            apply(relays.at[direction, j - 1], slot, put)

    def relay_hop(direction, h):
        for b in range(blocks):
            sum_copy(direction, h - 1, b).wait_recv()
            part_send[direction, h - 1, b] = (
                parts[direction, n_far - h, pl.ds(b * tile, tile), :]
                + part_recv[direction, h - 2, b].astype(jnp.float32)
            ).astype(jnp.bfloat16)
            sum_copy(direction, h, b).start()

    def near_block(b):
        live = live_ref[0, b]
        start = (r - reach) * blocks
        rows = pl.ds(b * tile, tile)
        for t in range(0, slots, 2):
            lhs = jnp.concatenate(
                [
                    (
                        near_t[b * slots + u].astype(jnp.float32)
                        * (u < live).astype(jnp.float32)
                    ).astype(jnp.bfloat16)
                    for u in (t, t + 1)
                ],
                axis=1,
            )
            places = [
                jnp.clip(cols_ref[0, b, u] - start, 0, (2 * reach + 1) * blocks - 1)
                for u in (t, t + 1)
            ]

            @pl.loop(0, width // COLS)
            def _(j):
                where = pl.ds(pl.multiple_of(j * COLS, COLS), COLS)
                rhs = jnp.concatenate([window[p, :, where] for p in places], axis=0)
                acc[rows, where] += jnp.dot(lhs, rhs, preferred_element_type=jnp.float32)

    loads[0].wait()

    @pl.loop(0, n_grp)
    def _(i):
        pack(i)

    for j in range(n_far, 0, -1):
        for direction in (0, 1):
            packet_copy(direction, j).start()

    acc[...] = jnp.zeros_like(acc)
    loads[1].wait()
    far_slot(own)

    loads[2].wait()
    for b in range(blocks):
        live = live_ref[0, b]
        total = jnp.zeros((tile, tile), jnp.float32)
        for t in range(slots):
            total = total + near_t[b * slots + t].astype(jnp.float32) * (t < live).astype(jnp.float32)
        for h in range(tiles_far):
            total = total + far_t[b * tiles_far + h].astype(jnp.float32)
        sums = jnp.sum(total, axis=1, keepdims=True)
        inv[pl.ds(b * tile, tile), :] = jnp.broadcast_to(1.0 / sums, (tile, tile))

    both = min(behind, ahead)

    @pl.loop(1, both)
    def _(k):
        for c in range(chunks):
            for direction in (0, 1):
                z_copy(direction, k, c).wait_recv()
                z_copy(direction, k + 1, c).start()
        far_slot(own - k)
        far_slot(own + k)

    for c in range(chunks):
        z_copy(0, both, c).wait_recv()
        z_copy(1, both, c).wait_recv()
        z_copy(1, both + 1, c).start()
    for j in range(1, n_far + 1):
        packet_copy(0, j).wait()
        packet_copy(1, j).wait()
    relay_first(0)
    relay_later(0)
    far_slot(own - both)
    far_slot(own + both)
    loads[3].wait()
    for d in steps:
        row_copy(d).wait()
    for b in range(blocks):
        near_block(b)

    for h in range(2, n_far):
        relay_hop(0, h)
    for c in range(chunks):
        z_copy(1, ahead, c).wait_recv()
    relay_first(1)
    relay_hop(0, n_far)
    relay_later(1)
    far_slot(own + ahead)
    for h in range(2, n_far):
        relay_hop(1, h)
    for b in range(blocks):
        sum_copy(0, n_far, b).wait_recv()
        acc[pl.ds(b * tile, tile), :] += part_recv[0, n_far - 1, b].astype(jnp.float32)
    relay_hop(1, n_far)

    for c in range(chunks):
        for direction in (0, 1):
            z_copy(direction, 1, c, first=True).wait_send()

    @pl.loop(1, both)
    def _(k):
        for c in range(chunks):
            for direction in (0, 1):
                z_copy(direction, k + 1, c).wait_send()

    for c in range(chunks):
        z_copy(1, ahead, c).wait_send()
    for h in range(1, n_far):
        for b in range(blocks):
            sum_copy(0, h, b).wait_send()
            sum_copy(1, h, b).wait_send()
    for b in range(blocks):
        sum_copy(0, n_far, b).wait_send()

    loads[4].wait()
    stores = []
    for b in range(blocks):
        rows = pl.ds(b * tile, tile)
        sum_copy(1, n_far, b).wait_recv()
        scale = jnp.concatenate([inv[rows, :]] * (width // tile), axis=1)
        mean[...] = (
            (acc[rows, :] + part_recv[1, n_far - 1, b].astype(jnp.float32)) * scale
        ).astype(jnp.bfloat16)

        @pl.loop(0, width // COLS)
        def _(j):
            where = pl.ds(pl.multiple_of(j * COLS, COLS), COLS)
            full = jnp.dot(mean[...], w_buf[:, where], preferred_element_type=jnp.float32)
            out_buf[rows, where] = jnp.maximum(full, 0.0).astype(jnp.bfloat16)

        stores.append(pltpu.make_async_copy(out_buf.at[rows], out.at[rows], load_sem.at[b]))
        stores[-1].start()
    for b in range(blocks):
        sum_copy(1, n_far, b).wait_send()
        stores[b].wait()


def solution(mesh):
    n_grp, n_row = mesh.shape["grp"], mesh.shape["row"]

    def body(
        features, history, weight, in_tiles, in_cols, tile_live, hist_tiles, hist_owner, hist_block
    ):
        tile = in_tiles.shape[3]
        rows, width = features.shape
        blocks = rows // tile
        shard = history.shape[0]
        chunks = shard // tile
        reach = (BAND + blocks - 1) // blocks
        behind, ahead, n_far = split_ring(n_grp)
        held = behind + 1 + ahead
        near = in_tiles.reshape(-1, tile, tile)
        far = hist_tiles.reshape(-1, tile, tile)
        smem = pl.BlockSpec(memory_space=pltpu.SMEM)
        hbm = pl.BlockSpec(memory_space=pl.ANY)
        bf16, f32 = jnp.bfloat16, jnp.float32
        dma = pltpu.SemaphoreType.DMA
        packet = 2 * tile + 16
        return pl.pallas_call(
            functools.partial(kernel, n_grp, n_row, reach),
            out_shape=jax.ShapeDtypeStruct((rows, width), bf16),
            in_specs=[smem] * 4 + [hbm] * 5,
            out_specs=hbm,
            scratch_shapes=[
                pltpu.VMEM((held, shard, width), bf16),
                pltpu.VMEM(((2 * reach + 1) * blocks, tile, width), bf16),
                pltpu.VMEM(weight.shape, bf16),
                pltpu.VMEM(near.shape, bf16),
                pltpu.VMEM(far.shape, bf16),
                pltpu.VMEM((rows, width), f32),
                pltpu.VMEM((rows, tile), f32),
                pltpu.VMEM((tile, width), bf16),
                pltpu.VMEM((rows, width), bf16),
                pltpu.VMEM((n_grp, packet, tile), bf16),
                pltpu.VMEM((2, n_far, packet, tile), bf16),
                pltpu.VMEM((2, n_far - 1, rows, width), f32),
                pltpu.VMEM((2, n_far, blocks, tile, width), bf16),
                pltpu.VMEM((2, n_far, blocks, tile, width), bf16),
                dma((5,)),
                dma((held, chunks)),
                dma((held, chunks)),
                dma((2, n_far)),
                dma((2, n_far)),
                dma((2, n_far, blocks)),
                dma((2, n_far, blocks)),
                dma((2 * reach,)),
                dma((2 * reach,)),
            ],
            compiler_params=pltpu.CompilerParams(
                collective_id=0, has_side_effects=True, vmem_limit_bytes=60 * 1024 * 1024
            ),
        )(
            in_cols, tile_live, hist_owner.reshape(-1), hist_block.reshape(-1),
            features.reshape(-1, tile, width), history, weight, near, far,
        )

    placed = (
        P(("grp", "row"), None),
        P(("grp", "row"), None),
        P(),
        P("grp", "row", None, None, None),
        P("grp", "row", None),
        P("grp", "row"),
        P("grp", "row", None, None, None),
        P(("grp", "row"), None),
        P(("grp", "row"), None),
    )
    return jax.shard_map(
        body, mesh=mesh, in_specs=placed, out_specs=P(("grp", "row"), None), check_vma=False
    )
```

```python
import functools

import jax
import jax.numpy as jnp
from jax import lax
from jax.experimental import pallas as pl
from jax.experimental.pallas import tpu as pltpu
from jax.sharding import PartitionSpec as P

MESH = pl.DeviceIdType.MESH
BAND = 6
COLS = 256


BEHIND, AHEAD, FAR_AHEAD = 4, 5, 3
PIECE = 128


def split_ring(n_grp):
    far = n_grp - 1 - BEHIND - AHEAD
    return (BEHIND, AHEAD), (far - FAR_AHEAD, FAR_AHEAD)


def kernel(
    n_grp, n_row, reach,
    cols_ref, live_ref, owner_ref, block_ref,
    feat, hist, near_in, far_in,
    out,
    ring, window, near_t, far_t, acc, inv,
    packets, relays, parts, part_send, part_recv,
    load_sem, z_send, z_recv, tile_send, tile_recv, sum_send, sum_recv, row_send, row_recv,
):
    g = lax.axis_index("grp")
    r = lax.axis_index("row")
    reached, n_far = split_ring(n_grp)
    behind, ahead = reached
    tile = near_t.shape[1]
    blocks, _, width = feat.shape
    chunks = hist.shape[0] // tile
    slots = near_t.shape[0] // blocks
    tiles_far = far_t.shape[0] // blocks
    requests = far_t.shape[0]
    own = behind
    pieces = acc.shape[0] // PIECE
    steps = [d for d in range(-reach, reach + 1) if d != 0]

    sign = 1 - 2 * lax.rem(r, 2)

    def at(distance):
        return lax.rem(g + sign * distance + 2 * n_grp, n_grp)

    def beside(d):
        return lax.rem(r + d + n_row, n_row)

    loads = [
        pltpu.make_async_copy(far_in, far_t, load_sem.at[0]),
        pltpu.make_async_copy(hist, ring.at[own], load_sem.at[1]),
        pltpu.make_async_copy(near_in, near_t, load_sem.at[2]),
        pltpu.make_async_copy(feat, window.at[pl.ds(reach * blocks, blocks)], load_sem.at[3]),
    ]
    for load in loads:
        load.start()

    barrier = pltpu.get_barrier_semaphore()
    partners = max(n_far)
    for j in range(1, partners + 1):
        for z in (at(-j), at(j)):
            pl.semaphore_signal(barrier, inc=1, device_id=(z, r), device_id_type=MESH)
    for d in steps:
        pl.semaphore_signal(barrier, inc=1, device_id=(g, beside(d)), device_id_type=MESH)
    pl.semaphore_wait(barrier, 2 * partners + len(steps))

    def slot_of(direction, k):
        return own - k if direction == 0 else own + k

    def towards(direction):
        return at(1) if direction == 0 else at(-1)

    def z_copy(direction, k, c, first=False):
        rows = pl.ds(c * tile, tile)
        slot = slot_of(direction, k)
        return pltpu.make_async_remote_copy(
            src_ref=hist.at[rows] if first else ring.at[slot_of(direction, k - 1), rows],
            dst_ref=ring.at[slot, rows],
            send_sem=z_send.at[slot, c],
            recv_sem=z_recv.at[slot, c],
            device_id=(towards(direction), r),
            device_id_type=MESH,
        )

    def packet_copy(direction, j):
        index = n_far[0] - j if direction == 0 else n_far[0] + own + ahead + j
        return pltpu.make_async_remote_copy(
            src_ref=packets.at[index],
            dst_ref=relays.at[direction, j - 1],
            send_sem=tile_send.at[direction, j - 1],
            recv_sem=tile_recv.at[direction, j - 1],
            device_id=(at(-j) if direction == 0 else at(j), r),
            device_id_type=MESH,
        )

    def sum_copy(direction, h, p):
        rows = pl.ds(p * PIECE, PIECE)
        return pltpu.make_async_remote_copy(
            src_ref=part_send.at[direction, h - 1, rows],
            dst_ref=part_recv.at[direction, h - 1, rows],
            send_sem=sum_send.at[direction, h - 1, p],
            recv_sem=sum_recv.at[direction, h - 1, p],
            device_id=(towards(direction), r),
            device_id_type=MESH,
        )

    def row_copy(d):
        i = steps.index(d)
        return pltpu.make_async_remote_copy(
            src_ref=feat,
            dst_ref=window.at[pl.ds((reach - d) * blocks, blocks)],
            send_sem=row_send.at[i],
            recv_sem=row_recv.at[i],
            device_id=(g, beside(d)),
            device_id_type=MESH,
        )

    for c in range(chunks):
        for direction in (0, 1):
            z_copy(direction, 1, c, first=True).start()
    for d in steps:
        row_copy(d).start()

    def pack(i):
        source = at(i - behind - n_far[0])
        count = jnp.int32(0)
        index = [jnp.int32(0), jnp.int32(0)]
        block = [jnp.int32(0), jnp.int32(0)]
        for h in range(requests):
            named = (owner_ref[h] == source).astype(jnp.int32)
            for c in range(2):
                taken = named * (count == c).astype(jnp.int32)
                index[c] = index[c] + taken * h
                block[c] = block[c] + taken * block_ref[h]
            count = count + named
        marks = []
        for c in range(2):
            alive = (count > c).astype(jnp.float32)
            packets[i, pl.ds(c * tile, tile), :] = (
                far_t[index[c]].astype(jnp.float32) * alive
            ).astype(jnp.bfloat16)
            marks += [index[c] // tiles_far, block[c]]
        row = lax.broadcasted_iota(jnp.int32, (16, tile), 0)
        rows = jnp.zeros((16, tile), jnp.int32)
        for n, mark in enumerate(marks):
            rows = rows + (row == n).astype(jnp.int32) * mark
        packets[i, pl.ds(2 * tile, 16), :] = rows.astype(jnp.float32).astype(jnp.bfloat16)

    def apply(packet, slot, put):
        marks = packet[pl.ds(2 * tile, 16), :].astype(jnp.float32).astype(jnp.int32)
        tops = [[] for _ in range(blocks)]
        numbers = []
        for c in range(2):
            values = packet[pl.ds(c * tile, tile), :].astype(jnp.float32)
            mine = marks[2 * c : 2 * c + 1, :]
            for b in range(blocks):
                keep = (mine == b).astype(jnp.float32)
                tops[b].append((values * keep).astype(jnp.bfloat16))
            numbers.append(
                jnp.broadcast_to(
                    jnp.concatenate([marks[2 * c + 1 : 2 * c + 2, :]] * (COLS // tile), axis=1),
                    (tile, COLS),
                )
            )
        lhs = jnp.concatenate([jnp.concatenate(top, axis=1) for top in tops], axis=0)

        @pl.loop(0, width // COLS)
        def _(j):
            where = pl.ds(pl.multiple_of(j * COLS, COLS), COLS)
            data = [ring[slot, pl.ds(p * tile, tile), where] for p in range(chunks)]
            taken = []
            for number in numbers:
                value = data[0]
                for p in range(1, chunks):
                    value = jnp.where(number == p, data[p], value)
                taken.append(value)
            rhs = jnp.concatenate(taken, axis=0)
            put(where, jnp.dot(lhs, rhs, preferred_element_type=jnp.float32))

    def far_slot(slot):
        def put(where, value):
            acc[:, where] += value

        apply(packets.at[slot + n_far[0]], slot, put)

    def relay_slot(direction):
        return 0 if direction == 0 else own + ahead

    def relay_first(direction):
        def put(where, value):
            part_send[direction, 0, :, where] = value.astype(jnp.bfloat16)

        for j in range(1, n_far[direction] + 1):
            packet_copy(direction, j).wait()
        apply(relays.at[direction, n_far[direction] - 1], relay_slot(direction), put)
        for p in range(pieces):
            sum_copy(direction, 1, p).start()

    def relay_part(direction, j):
        def put(where, value):
            parts[direction, j - 1, :, where] = value

        apply(relays.at[direction, j - 1], relay_slot(direction), put)

    def take_hop(direction, h, p):
        rows = pl.ds(p * PIECE, PIECE)
        sum_copy(direction, h, p).wait_recv()
        came = part_recv[direction, h - 1, rows].astype(jnp.float32)
        if h < n_far[direction]:
            part_send[direction, h, rows] = (
                parts[direction, n_far[direction] - h - 1, rows, :] + came
            ).astype(jnp.bfloat16)
            sum_copy(direction, h + 1, p).start()
        else:
            acc[rows, :] += came

    def near_block(b):
        live = live_ref[0, b]
        start = (r - reach) * blocks
        rows = pl.ds(b * tile, tile)
        for t in range(0, slots, 2):
            lhs = jnp.concatenate(
                [
                    (
                        near_t[b * slots + u].astype(jnp.float32)
                        * (u < live).astype(jnp.float32)
                    ).astype(jnp.bfloat16)
                    for u in (t, t + 1)
                ],
                axis=1,
            )
            places = [
                jnp.clip(cols_ref[0, b, u] - start, 0, (2 * reach + 1) * blocks - 1)
                for u in (t, t + 1)
            ]

            @pl.loop(0, width // COLS)
            def _(j):
                where = pl.ds(pl.multiple_of(j * COLS, COLS), COLS)
                rhs = jnp.concatenate([window[p, :, where] for p in places], axis=0)
                acc[rows, where] += jnp.dot(lhs, rhs, preferred_element_type=jnp.float32)

    loads[0].wait()

    @pl.loop(0, n_grp)
    def _(i):
        pack(i)

    for j in range(partners, 0, -1):
        for direction in (0, 1):
            if j <= n_far[direction]:
                packet_copy(direction, j).start()

    acc[...] = jnp.zeros_like(acc)
    loads[1].wait()
    far_slot(own)

    loads[2].wait()
    for b in range(blocks):
        live = live_ref[0, b]
        total = jnp.zeros((tile, tile), jnp.float32)
        for t in range(slots):
            total = total + near_t[b * slots + t].astype(jnp.float32) * (t < live).astype(jnp.float32)
        for h in range(tiles_far):
            total = total + far_t[b * tiles_far + h].astype(jnp.float32)
        sums = jnp.sum(total, axis=1, keepdims=True)
        inv[pl.ds(b * tile, tile), :] = jnp.broadcast_to(1.0 / sums, (tile, tile))

    both = min(behind, ahead)

    @pl.loop(1, both)
    def _(k):
        for c in range(chunks):
            for direction in (0, 1):
                z_copy(direction, k, c).wait_recv()
                z_copy(direction, k + 1, c).start()
        far_slot(own - k)
        far_slot(own + k)

    loads[3].wait()
    for d in steps:
        row_copy(d).wait()
    for b in range(blocks):
        near_block(b)

    events = {}
    begin = [n_far[1 - d] * (n_far[1 - d] + 1) for d in (0, 1)]
    for direction in (0, 1):
        for k in range(both, reached[direction] + 1):
            events.setdefault(begin[direction] + 24 * k, []).append((direction, "shard", k))
        for h in range(1, n_far[direction] + 1):
            events.setdefault(
                begin[direction] + 24 * reached[direction] + 16 * h, []
            ).append((direction, "sum", h))
    ends = [begin[d] + 24 * reached[d] + 16 * n_far[d] for d in (0, 1)]
    last = 0 if ends[0] > ends[1] else 1
    parts_left = {0: [], 1: []}
    slots_left = []
    for when in sorted(events):
        shards = [(d, n) for d, kind, n in events[when] if kind == "shard"]
        sums = [(d, n) for d, kind, n in events[when] if kind == "sum"]
        for c in range(chunks):
            for d, k in shards:
                z_copy(d, k, c).wait_recv()
                if k < reached[d]:
                    z_copy(d, k + 1, c).start()
        for d, k in shards:
            if k == reached[d]:
                relay_first(d)
                parts_left[d] = list(range(n_far[d] - 1, 0, -1))
            slots_left.append(slot_of(d, k))
        for p in range(pieces):
            for d, h in sums:
                if (d, h) != (last, n_far[last]):
                    take_hop(d, h, p)
        for d in (0, 1):
            if parts_left[d]:
                relay_part(d, parts_left[d].pop(0))
        if slots_left:
            far_slot(slots_left.pop(0))
    for slot in slots_left:
        far_slot(slot)

    for c in range(chunks):
        for direction in (0, 1):
            z_copy(direction, 1, c, first=True).wait_send()

    @pl.loop(1, both)
    def _(k):
        for c in range(chunks):
            for direction in (0, 1):
                z_copy(direction, k + 1, c).wait_send()

    for direction in (0, 1):
        for k in range(both, reached[direction]):
            for c in range(chunks):
                z_copy(direction, k + 1, c).wait_send()
        for h in range(1, n_far[direction] + 1):
            if (direction, h) != (last, n_far[last]):
                for p in range(pieces):
                    sum_copy(direction, h, p).wait_send()

    for p in range(pieces):
        rows = pl.ds(p * PIECE, PIECE)
        sum_copy(last, n_far[last], p).wait_recv()
        scale = jnp.concatenate([inv[rows, :]] * (width // tile), axis=1)
        out[rows, :] = (
            (acc[rows, :] + part_recv[last, n_far[last] - 1, rows].astype(jnp.float32)) * scale
        ).astype(jnp.bfloat16)
    for p in range(pieces):
        sum_copy(last, n_far[last], p).wait_send()


def solution(mesh):
    n_grp, n_row = mesh.shape["grp"], mesh.shape["row"]

    def body(
        features, history, weight, in_tiles, in_cols, tile_live, hist_tiles, hist_owner, hist_block
    ):
        tile = in_tiles.shape[3]
        rows, width = features.shape
        blocks = rows // tile
        shard = history.shape[0]
        chunks = shard // tile
        reach = (BAND + blocks - 1) // blocks
        reached, n_far = split_ring(n_grp)
        most = max(n_far)
        held = sum(reached) + 1
        pieces = rows // PIECE
        near = in_tiles.reshape(-1, tile, tile)
        far = hist_tiles.reshape(-1, tile, tile)
        smem = pl.BlockSpec(memory_space=pltpu.SMEM)
        hbm = pl.BlockSpec(memory_space=pl.ANY)
        bf16, f32 = jnp.bfloat16, jnp.float32
        dma = pltpu.SemaphoreType.DMA
        packet = 2 * tile + 16
        kept = [
            pltpu.with_memory_space_constraint(x, pltpu.HBM)
            for x in (
                in_cols, tile_live, hist_owner.reshape(-1), hist_block.reshape(-1),
                features.reshape(-1, tile, width), history, near, far,
            )
        ]
        means = pl.pallas_call(
            functools.partial(kernel, n_grp, n_row, reach),
            out_shape=pltpu.VMEM((rows, width), bf16),
            in_specs=[smem] * 4 + [hbm] * 4,
            out_specs=pl.BlockSpec(memory_space=pltpu.VMEM),
            scratch_shapes=[
                pltpu.VMEM((held, shard, width), bf16),
                pltpu.VMEM(((2 * reach + 1) * blocks, tile, width), bf16),
                pltpu.VMEM(near.shape, bf16),
                pltpu.VMEM(far.shape, bf16),
                pltpu.VMEM((rows, width), f32),
                pltpu.VMEM((rows, tile), f32),
                pltpu.VMEM((n_grp, packet, tile), bf16),
                pltpu.VMEM((2, most, packet, tile), bf16),
                pltpu.VMEM((2, most - 1, rows, width), f32),
                pltpu.VMEM((2, most, rows, width), bf16),
                pltpu.VMEM((2, most, rows, width), bf16),
                dma((4,)),
                dma((held, chunks)),
                dma((held, chunks)),
                dma((2, most)),
                dma((2, most)),
                dma((2, most, pieces)),
                dma((2, most, pieces)),
                dma((2 * reach,)),
                dma((2 * reach,)),
            ],
            compiler_params=pltpu.CompilerParams(
                collective_id=0, has_side_effects=True, vmem_limit_bytes=48 * 1024 * 1024
            ),
        )(*kept)
        return jax.nn.relu(jnp.dot(means, weight, preferred_element_type=f32)).astype(bf16)

    placed = (
        P(("grp", "row"), None),
        P(("grp", "row"), None),
        P(),
        P("grp", "row", None, None, None),
        P("grp", "row", None),
        P("grp", "row"),
        P("grp", "row", None, None, None),
        P(("grp", "row"), None),
        P(("grp", "row"), None),
    )
    return jax.shard_map(
        body, mesh=mesh, in_specs=placed, out_specs=P(("grp", "row"), None), check_vma=False
    )
```

```python
import functools

import jax
import jax.numpy as jnp
from jax import lax
from jax.experimental import pallas as pl
from jax.experimental.pallas import tpu as pltpu
from jax.sharding import PartitionSpec as P

MESH = pl.DeviceIdType.MESH
BAND = 6
COLS = 256


BEHIND, AHEAD, FAR_AHEAD = 4, 5, 3
PIECE = 128


def split_ring(n_grp):
    far = n_grp - 1 - BEHIND - AHEAD
    return (BEHIND, AHEAD), (far - FAR_AHEAD, FAR_AHEAD)


def kernel(
    n_grp, n_row, reach,
    cols_in, live_in, owner_in, block_in,
    feat, hist, near_in, far_in,
    out,
    cols_ref, live_ref, owner_ref, block_ref,
    ring, window, near_t, far_t, acc, inv,
    packets, relays, parts, part_send, part_recv,
    load_sem, table_sem, z_send, z_recv, tile_send, tile_recv, sum_send, sum_recv, row_send, row_recv,
):
    g = lax.axis_index("grp")
    r = lax.axis_index("row")
    reached, n_far = split_ring(n_grp)
    behind, ahead = reached
    tile = near_t.shape[1]
    blocks, _, width = feat.shape
    chunks = hist.shape[0] // tile
    slots = near_t.shape[0] // blocks
    tiles_far = far_t.shape[0] // blocks
    requests = far_t.shape[0]
    own = behind
    pieces = acc.shape[0] // PIECE
    steps = [d for d in range(-reach, reach + 1) if d != 0]

    sign = 1 - 2 * lax.rem(r, 2)

    def at(distance):
        return lax.rem(g + sign * distance + 2 * n_grp, n_grp)

    def beside(d):
        return lax.rem(r + d + n_row, n_row)

    loads = [
        pltpu.make_async_copy(far_in, far_t, load_sem.at[0]),
        pltpu.make_async_copy(hist, ring.at[own], load_sem.at[1]),
        pltpu.make_async_copy(near_in, near_t, load_sem.at[2]),
        pltpu.make_async_copy(feat, window.at[pl.ds(reach * blocks, blocks)], load_sem.at[3]),
    ]
    tables = [
        pltpu.make_async_copy(source, table, table_sem.at[i])
        for i, (source, table) in enumerate(
            ((owner_in, owner_ref), (block_in, block_ref), (live_in, live_ref), (cols_in, cols_ref))
        )
    ]

    barrier = pltpu.get_barrier_semaphore()
    partners = max(n_far)
    for j in range(1, partners + 1):
        for z in (at(-j), at(j)):
            pl.semaphore_signal(barrier, inc=1, device_id=(z, r), device_id_type=MESH)
    for d in steps:
        pl.semaphore_signal(barrier, inc=1, device_id=(g, beside(d)), device_id_type=MESH)
    pl.semaphore_wait(barrier, 2 * partners + len(steps))

    def slot_of(direction, k):
        return own - k if direction == 0 else own + k

    def towards(direction):
        return at(1) if direction == 0 else at(-1)

    def z_copy(direction, k, c, first=False):
        rows = pl.ds(c * tile, tile)
        slot = slot_of(direction, k)
        return pltpu.make_async_remote_copy(
            src_ref=hist.at[rows] if first else ring.at[slot_of(direction, k - 1), rows],
            dst_ref=ring.at[slot, rows],
            send_sem=z_send.at[slot, c],
            recv_sem=z_recv.at[slot, c],
            device_id=(towards(direction), r),
            device_id_type=MESH,
        )

    def packet_copy(direction, j):
        index = n_far[0] - j if direction == 0 else n_far[0] + own + ahead + j
        return pltpu.make_async_remote_copy(
            src_ref=packets.at[index],
            dst_ref=relays.at[direction, j - 1],
            send_sem=tile_send.at[direction, j - 1],
            recv_sem=tile_recv.at[direction, j - 1],
            device_id=(at(-j) if direction == 0 else at(j), r),
            device_id_type=MESH,
        )

    def sum_copy(direction, h, p):
        rows = pl.ds(p * PIECE, PIECE)
        return pltpu.make_async_remote_copy(
            src_ref=part_send.at[direction, h - 1, rows],
            dst_ref=part_recv.at[direction, h - 1, rows],
            send_sem=sum_send.at[direction, h - 1, p],
            recv_sem=sum_recv.at[direction, h - 1, p],
            device_id=(towards(direction), r),
            device_id_type=MESH,
        )

    def row_copy(d):
        i = steps.index(d)
        return pltpu.make_async_remote_copy(
            src_ref=feat,
            dst_ref=window.at[pl.ds((reach - d) * blocks, blocks)],
            send_sem=row_send.at[i],
            recv_sem=row_recv.at[i],
            device_id=(g, beside(d)),
            device_id_type=MESH,
        )

    for c in range(chunks):
        for direction in (0, 1):
            z_copy(direction, 1, c, first=True).start()
    for load in loads + tables:
        load.start()
    for d in steps:
        row_copy(d).start()

    def pack(i):
        source = at(i - behind - n_far[0])
        count = jnp.int32(0)
        index = [jnp.int32(0), jnp.int32(0)]
        block = [jnp.int32(0), jnp.int32(0)]
        for h in range(requests):
            named = (owner_ref[h] == source).astype(jnp.int32)
            for c in range(2):
                taken = named * (count == c).astype(jnp.int32)
                index[c] = index[c] + taken * h
                block[c] = block[c] + taken * block_ref[h]
            count = count + named
        marks = []
        for c in range(2):
            alive = (count > c).astype(jnp.float32)
            packets[i, pl.ds(c * tile, tile), :] = (
                far_t[index[c]].astype(jnp.float32) * alive
            ).astype(jnp.bfloat16)
            marks += [index[c] // tiles_far, block[c]]
        row = lax.broadcasted_iota(jnp.int32, (16, tile), 0)
        rows = jnp.zeros((16, tile), jnp.int32)
        for n, mark in enumerate(marks):
            rows = rows + (row == n).astype(jnp.int32) * mark
        packets[i, pl.ds(2 * tile, 16), :] = rows.astype(jnp.float32).astype(jnp.bfloat16)

    def apply(packet, slot, put):
        marks = packet[pl.ds(2 * tile, 16), :].astype(jnp.float32).astype(jnp.int32)
        tops = [[] for _ in range(blocks)]
        numbers = []
        for c in range(2):
            values = packet[pl.ds(c * tile, tile), :].astype(jnp.float32)
            mine = marks[2 * c : 2 * c + 1, :]
            for b in range(blocks):
                keep = (mine == b).astype(jnp.float32)
                tops[b].append((values * keep).astype(jnp.bfloat16))
            numbers.append(
                jnp.broadcast_to(
                    jnp.concatenate([marks[2 * c + 1 : 2 * c + 2, :]] * (COLS // tile), axis=1),
                    (tile, COLS),
                )
            )
        lhs = jnp.concatenate([jnp.concatenate(top, axis=1) for top in tops], axis=0)

        @pl.loop(0, width // COLS)
        def _(j):
            where = pl.ds(pl.multiple_of(j * COLS, COLS), COLS)
            data = [ring[slot, pl.ds(p * tile, tile), where] for p in range(chunks)]
            taken = []
            for number in numbers:
                value = data[0]
                for p in range(1, chunks):
                    value = jnp.where(number == p, data[p], value)
                taken.append(value)
            rhs = jnp.concatenate(taken, axis=0)
            put(where, jnp.dot(lhs, rhs, preferred_element_type=jnp.float32))

    def far_slot(slot):
        def put(where, value):
            acc[:, where] += value

        apply(packets.at[slot + n_far[0]], slot, put)

    def relay_slot(direction):
        return 0 if direction == 0 else own + ahead

    def relay_first(direction):
        def put(where, value):
            part_send[direction, 0, :, where] = value.astype(jnp.bfloat16)

        for j in range(1, n_far[direction] + 1):
            packet_copy(direction, j).wait()
        apply(relays.at[direction, n_far[direction] - 1], relay_slot(direction), put)
        for p in range(pieces):
            sum_copy(direction, 1, p).start()

    def relay_part(direction, j):
        def put(where, value):
            parts[direction, j - 1, :, where] = value

        apply(relays.at[direction, j - 1], relay_slot(direction), put)

    def take_hop(direction, h, p):
        rows = pl.ds(p * PIECE, PIECE)
        sum_copy(direction, h, p).wait_recv()
        came = part_recv[direction, h - 1, rows].astype(jnp.float32)
        if h < n_far[direction]:
            part_send[direction, h, rows] = (
                parts[direction, n_far[direction] - h - 1, rows, :] + came
            ).astype(jnp.bfloat16)
            sum_copy(direction, h + 1, p).start()
        else:
            acc[rows, :] += came

    def near_block(b):
        live = live_ref[0, b]
        start = (r - reach) * blocks
        rows = pl.ds(b * tile, tile)
        for t in range(0, slots, 2):
            lhs = jnp.concatenate(
                [
                    (
                        near_t[b * slots + u].astype(jnp.float32)
                        * (u < live).astype(jnp.float32)
                    ).astype(jnp.bfloat16)
                    for u in (t, t + 1)
                ],
                axis=1,
            )
            places = [
                jnp.clip(cols_ref[0, b, u] - start, 0, (2 * reach + 1) * blocks - 1)
                for u in (t, t + 1)
            ]

            @pl.loop(0, width // COLS)
            def _(j):
                where = pl.ds(pl.multiple_of(j * COLS, COLS), COLS)
                rhs = jnp.concatenate([window[p, :, where] for p in places], axis=0)
                acc[rows, where] += jnp.dot(lhs, rhs, preferred_element_type=jnp.float32)

    loads[0].wait()
    for table in tables:
        table.wait()

    @pl.loop(0, n_grp)
    def _(i):
        pack(i)

    for j in range(partners, 0, -1):
        for direction in (0, 1):
            if j <= n_far[direction]:
                packet_copy(direction, j).start()

    acc[...] = jnp.zeros_like(acc)
    loads[1].wait()
    far_slot(own)

    loads[2].wait()
    for b in range(blocks):
        live = live_ref[0, b]
        total = jnp.zeros((tile, tile), jnp.float32)
        for t in range(slots):
            total = total + near_t[b * slots + t].astype(jnp.float32) * (t < live).astype(jnp.float32)
        for h in range(tiles_far):
            total = total + far_t[b * tiles_far + h].astype(jnp.float32)
        sums = jnp.sum(total, axis=1, keepdims=True)
        inv[pl.ds(b * tile, tile), :] = jnp.broadcast_to(1.0 / sums, (tile, tile))

    both = min(behind, ahead)

    @pl.loop(1, both)
    def _(k):
        for c in range(chunks):
            for direction in (0, 1):
                z_copy(direction, k, c).wait_recv()
                z_copy(direction, k + 1, c).start()
        far_slot(own - k)
        far_slot(own + k)

    loads[3].wait()
    for d in steps:
        row_copy(d).wait()
    for b in range(blocks):
        near_block(b)

    events = {}
    begin = [n_far[1 - d] * (n_far[1 - d] + 1) for d in (0, 1)]
    for direction in (0, 1):
        for k in range(both, reached[direction] + 1):
            events.setdefault(begin[direction] + 24 * k, []).append((direction, "shard", k))
        for h in range(1, n_far[direction] + 1):
            events.setdefault(
                begin[direction] + 24 * reached[direction] + 16 * h, []
            ).append((direction, "sum", h))
    ends = [begin[d] + 24 * reached[d] + 16 * n_far[d] for d in (0, 1)]
    last = 0 if ends[0] > ends[1] else 1
    parts_left = {0: [], 1: []}
    slots_left = []
    for when in sorted(events):
        shards = [(d, n) for d, kind, n in events[when] if kind == "shard"]
        sums = [(d, n) for d, kind, n in events[when] if kind == "sum"]
        for c in range(chunks):
            for d, k in shards:
                z_copy(d, k, c).wait_recv()
                if k < reached[d]:
                    z_copy(d, k + 1, c).start()
        for d, k in shards:
            if k == reached[d]:
                relay_first(d)
                parts_left[d] = list(range(n_far[d] - 1, 0, -1))
            slots_left.append(slot_of(d, k))
        for p in range(pieces):
            for d, h in sums:
                if (d, h) != (last, n_far[last]):
                    take_hop(d, h, p)
        for d in (0, 1):
            if parts_left[d]:
                relay_part(d, parts_left[d].pop(0))
        if slots_left:
            far_slot(slots_left.pop(0))
    for slot in slots_left:
        far_slot(slot)

    for c in range(chunks):
        for direction in (0, 1):
            z_copy(direction, 1, c, first=True).wait_send()

    @pl.loop(1, both)
    def _(k):
        for c in range(chunks):
            for direction in (0, 1):
                z_copy(direction, k + 1, c).wait_send()

    for direction in (0, 1):
        for k in range(both, reached[direction]):
            for c in range(chunks):
                z_copy(direction, k + 1, c).wait_send()
        for h in range(1, n_far[direction] + 1):
            if (direction, h) != (last, n_far[last]):
                for p in range(pieces):
                    sum_copy(direction, h, p).wait_send()

    for p in range(pieces):
        rows = pl.ds(p * PIECE, PIECE)
        sum_copy(last, n_far[last], p).wait_recv()
        scale = jnp.concatenate([inv[rows, :]] * (width // tile), axis=1)
        out[rows, :] = (
            (acc[rows, :] + part_recv[last, n_far[last] - 1, rows].astype(jnp.float32)) * scale
        ).astype(jnp.bfloat16)
    for p in range(pieces):
        sum_copy(last, n_far[last], p).wait_send()


def solution(mesh):
    n_grp, n_row = mesh.shape["grp"], mesh.shape["row"]

    def body(
        features, history, weight, in_tiles, in_cols, tile_live, hist_tiles, hist_owner, hist_block
    ):
        tile = in_tiles.shape[3]
        rows, width = features.shape
        blocks = rows // tile
        shard = history.shape[0]
        chunks = shard // tile
        reach = (BAND + blocks - 1) // blocks
        reached, n_far = split_ring(n_grp)
        most = max(n_far)
        held = sum(reached) + 1
        pieces = rows // PIECE
        near = in_tiles.reshape(-1, tile, tile)
        far = hist_tiles.reshape(-1, tile, tile)
        hbm = pl.BlockSpec(memory_space=pl.ANY)
        bf16, f32 = jnp.bfloat16, jnp.float32
        dma = pltpu.SemaphoreType.DMA
        packet = 2 * tile + 16
        kept = [
            pltpu.with_memory_space_constraint(x, pltpu.HBM)
            for x in (
                in_cols, tile_live, hist_owner.reshape(-1), hist_block.reshape(-1),
                features.reshape(-1, tile, width), history, near, far,
            )
        ]
        means = pl.pallas_call(
            functools.partial(kernel, n_grp, n_row, reach),
            out_shape=pltpu.VMEM((rows, width), bf16),
            in_specs=[hbm] * 8,
            out_specs=pl.BlockSpec(memory_space=pltpu.VMEM),
            scratch_shapes=[
                *[pltpu.SMEM(x.shape, jnp.int32) for x in kept[:4]],
                pltpu.VMEM((held, shard, width), bf16),
                pltpu.VMEM(((2 * reach + 1) * blocks, tile, width), bf16),
                pltpu.VMEM(near.shape, bf16),
                pltpu.VMEM(far.shape, bf16),
                pltpu.VMEM((rows, width), f32),
                pltpu.VMEM((rows, tile), f32),
                pltpu.VMEM((n_grp, packet, tile), bf16),
                pltpu.VMEM((2, most, packet, tile), bf16),
                pltpu.VMEM((2, most - 1, rows, width), f32),
                pltpu.VMEM((2, most, rows, width), bf16),
                pltpu.VMEM((2, most, rows, width), bf16),
                dma((4,)),
                dma((4,)),
                dma((held, chunks)),
                dma((held, chunks)),
                dma((2, most)),
                dma((2, most)),
                dma((2, most, pieces)),
                dma((2, most, pieces)),
                dma((2 * reach,)),
                dma((2 * reach,)),
            ],
            compiler_params=pltpu.CompilerParams(
                collective_id=0, has_side_effects=True, vmem_limit_bytes=48 * 1024 * 1024
            ),
        )(*kept)
        return jax.nn.relu(jnp.dot(means, weight, preferred_element_type=f32)).astype(bf16)

    placed = (
        P(("grp", "row"), None),
        P(("grp", "row"), None),
        P(),
        P("grp", "row", None, None, None),
        P("grp", "row", None),
        P("grp", "row"),
        P("grp", "row", None, None, None),
        P(("grp", "row"), None),
        P(("grp", "row"), None),
    )
    return jax.shard_map(
        body, mesh=mesh, in_specs=placed, out_specs=P(("grp", "row"), None), check_vma=False
    )
```
